32 devices in a mesh: dp: 2 (over x), expert: 16 (over z, y, core).
Axes of the slice: x: 2, y: 2, z: 4, core: 2. Of those that a mesh axis runs over, the one named last changes fastest.
Arguments:
- tokens: bfloat16 [4096, 1024], P(('dp', 'expert')), may hold values from -6 to 6
- routes: int32 [4096, 6], P(('dp', 'expert')), may hold values from 0 to 15, all different within a row; in each aligned block of 128 rows (0 to 127, 128 to 255, ...) at most 96 rows name the same one
- route_weights: float32 [4096, 6], P(('dp', 'expert')), may hold values from 0.1 to 1
- gate_weight: bfloat16 [16, 1024, 512], P('expert'), may hold values from -0.1875 to 0.1875
- up_weight: bfloat16 [16, 1024, 512], P('expert'), may hold values from -0.1875 to 0.1875
- down_weight: bfloat16 [16, 512, 1024], P('expert'), may hold values from -0.25 to 0.25
- cotangent: bfloat16 [4096, 1024], P(('dp', 'expert')), may hold values from -3 to 3
Outputs:
- mixed_latent: bfloat16 [4096, 1024], P(('dp', 'expert'))
- latent_grad: bfloat16 [4096, 1024], P(('dp', 'expert'))
- gate_grad: float32 [16, 1024, 512], P('expert', 'dp')
- up_grad: float32 [16, 1024, 512], P('expert', 'dp')
- down_grad: float32 [16, 512, 1024], P('expert', None, 'dp')
The draws below stay inside these ranges and needn't reach their ends.
Inputs may be any that keep to these rules, and one draw needn't show every extreme that they name: `routes`: each row names 6 different experts. In each aligned block of 128 rows (the rows of one device) no expert is named by more than 96 rows, and some expert is named by exactly 96 rows in some block.
All inputs are finite; a program needn't handle non-finite values.
Results may differ from the reference program's by a relative error of at most 0.015.
Values may be sent and summed in bfloat16 or wider, within the bound.
A program may use at most 64 MiB of HBM per device.

```python
import math
import jax
import jax.numpy as jnp
import numpy as np
from jax import lax

LATENT = 1024
FFN = 512
TOP = 6
TOK_DEV = 128
EXPERTS = 16
CAPACITY = 48
TOKENS = 4096
N_DP = 2
N_EXPERT = 16


def level_of(key, extent, shards, low, top_value):
    gain, own = 1.0, jax.random.fold_in(key, 6)
    for axis_at, parts in shards:
        heights = jnp.exp(jax.random.uniform(jax.random.fold_in(own, axis_at), (parts,), jnp.float32, low / len(shards), top_value / len(shards)))
        gain = gain * jnp.repeat(heights, extent[axis_at] // parts).reshape([-1 if axis == axis_at else 1 for axis in range(len(extent))])
    return gain


def routed_block(key, own, number, rows, count, top, reach, skew):
    sequence = jax.random.permutation(key, count)
    crowded, usual = portions_of(count, rows * top, reach, skew, True), portions_of(count, rows * top, reach, skew, False)
    places = jnp.arange(count)

    def named(tallies, turn):
        used = int((tallies > 0).sum())
        fixed = max(1, used // 4)
        shifted = fixed + (places - fixed + turn * (used - fixed)) % max(1, count - fixed)
        return jnp.zeros((count,), jnp.int32).at[sequence[jnp.where(places < fixed, places, shifted)]].set(jnp.asarray(tallies, jnp.int32))

    tallies = jnp.where(number % 4 == 0, named(crowded, number // 4), named(usual, number - number // 4 - 1))
    mixed = jax.random.permutation(jax.random.fold_in(own, 3), count)
    giver, sink = mixed[0:count // 2 * 2:2], mixed[1:count // 2 * 2:2]
    slack = jnp.minimum(tallies[giver] - 1, reach - tallies[sink]) // 2
    slack = jnp.where((giver == sequence[0]) | (sink == sequence[0]) | (tallies[sink] == 0), 0, jnp.maximum(slack, 0))
    shifted = jax.random.randint(jax.random.fold_in(own, 4), (count // 2,), 0, 1 << 20) % (slack + 1)
    tallies = tallies.at[giver].add(-shifted).at[sink].add(shifted)
    items = jnp.searchsorted(jnp.cumsum(tallies), jnp.arange(rows * top), side="right").astype(jnp.int32)
    grid = items.reshape(top, rows).T
    grid = grid[jax.random.permutation(jax.random.fold_in(own, 1), rows)]
    turn = jax.random.randint(jax.random.fold_in(own, 2), (rows, 1), 0, top)
    return jnp.take_along_axis(grid, (jnp.arange(top)[None, :] + turn) % top, axis=1)


def portions_of(count, total, most, lean, full):
    loads = [(1 << 20) // math.isqrt(grade ** lean) + 1 for grade in range(1, count + 1)]
    largest = most if full else min(most, max(-(-total // count), total * loads[0] // sum(loads)))
    least = 1 if total - largest >= count - 1 else 0
    given, spare = [largest] + [least] * (count - 1), total - largest - least * (count - 1)
    while spare > 0:
        movable = [i for i in range(1, count) if given[i] < largest] or [i for i in range(1, count) if given[i] < most]
        whole, budget = sum([loads[i] for i in movable]), spare
        for i in movable:
            addition = min(most - given[i], max(1, budget * loads[i] // whole), spare)
            given[i] = given[i] + addition
            spare = spare - addition
    return np.array(given)


def noise(own_key, extent, width, limit, split=(), kind=jnp.bfloat16):
    values = width * jax.random.normal(own_key, extent, jnp.float32)
    if split:
        values = values * level_of(own_key, extent, split, -0.22, 0.18)
    return jnp.clip(values, -limit, limit).astype(kind)


def setup_inputs(seed: int = 0) -> dict:
    seeds = jax.random.split(jax.random.key(seed), 8)
    tokens = noise(seeds[0], (TOKENS, LATENT), 1.0, 6.0, ((0, 32),))
    routes_keys = jax.random.split(jax.random.fold_in(seeds[1], 1), TOKENS // TOK_DEV)
    routes_turns = jax.random.permutation(jax.random.fold_in(seeds[1], 3), TOKENS // TOK_DEV)
    routes = jax.vmap(lambda own, number: routed_block(jax.random.fold_in(seeds[1], 2), own, number, TOK_DEV, EXPERTS, TOP, 2 * CAPACITY, 2))(routes_keys, routes_turns).reshape((TOKENS, TOP))
    route_weights = jnp.clip(jnp.exp(math.log(1.0) - 2.3025851 * jax.random.uniform(seeds[2], (TOKENS, TOP), jnp.float32) ** level_of(seeds[2], (TOKENS, TOP), ((0, 32),), -0.2, 0.2)), 0.1, 1.0)
    gate_weight = noise(seeds[3], (EXPERTS, LATENT, FFN), LATENT ** -0.5, 0.1875, ((0, 16),))
    up_weight = noise(seeds[4], (EXPERTS, LATENT, FFN), LATENT ** -0.5, 0.1875, ((0, 16),))
    down_weight = noise(seeds[5], (EXPERTS, FFN, LATENT), FFN ** -0.5, 0.25, ((0, 16),))
    cotangent = noise(seeds[6], (TOKENS, LATENT), 0.5, 3.0, ((0, 32),))
    return dict(tokens=tokens, routes=routes, route_weights=route_weights, gate_weight=gate_weight, up_weight=up_weight, down_weight=down_weight, cotangent=cotangent)


def slot_plan(route_rows, experts, capacity):
    flat_routes = route_rows.reshape(-1)
    one_hot = (flat_routes[:, None] == jnp.arange(experts, dtype=jnp.int32)[None, :]).astype(jnp.int32)
    earlier = jnp.cumsum(one_hot, axis=0) - one_hot
    slot_rank = jnp.sum(earlier * one_hot, axis=1)
    kept_mask = slot_rank < capacity
    slot_index = jnp.where(kept_mask, flat_routes * capacity + slot_rank, experts * capacity).astype(jnp.int32)
    return kept_mask, slot_index


def pack_rows(row_values, slot_index, experts, capacity):
    latent_width = row_values.shape[1]
    buffer = jnp.zeros((experts * capacity + 1, latent_width), row_values.dtype)
    buffer = buffer.at[slot_index].set(row_values)
    return buffer[:-1].reshape(experts, capacity, latent_width)


def unpack_rows(buffer, slot_index, top_count):
    latent_width = buffer.shape[-1]
    padded = jnp.concatenate([buffer.reshape(-1, latent_width), jnp.zeros((1, latent_width), buffer.dtype)], axis=0)
    return padded[slot_index].reshape(-1, top_count, latent_width)


def expert_forward(inputs, gate_matrix, up_matrix, down_matrix):
    gate_pre = jnp.dot(inputs, gate_matrix, preferred_element_type=jnp.float32)
    up_pre = jnp.dot(inputs, up_matrix, preferred_element_type=jnp.float32)
    hidden = (jax.nn.silu(gate_pre) * up_pre).astype(jnp.bfloat16)
    outputs = jnp.dot(hidden, down_matrix, preferred_element_type=jnp.float32).astype(jnp.bfloat16)
    return outputs, gate_pre, up_pre, hidden


def expert_backward(out_grads, gate_pre, up_pre, gate_matrix, up_matrix, down_matrix):
    contract_last = (((1,), (1,)), ((), ()))
    hidden_grad = lax.dot_general(out_grads, down_matrix, contract_last, preferred_element_type=jnp.float32)
    sigmoid_gate = jax.nn.sigmoid(gate_pre)
    up_grad_pre = (hidden_grad * gate_pre * sigmoid_gate).astype(jnp.bfloat16)
    gate_grad_pre = (hidden_grad * up_pre * sigmoid_gate * (1.0 + gate_pre * (1.0 - sigmoid_gate))).astype(jnp.bfloat16)
    input_grads = lax.dot_general(gate_grad_pre, gate_matrix, contract_last, preferred_element_type=jnp.float32)
    input_grads = input_grads + lax.dot_general(up_grad_pre, up_matrix, contract_last, preferred_element_type=jnp.float32)
    return input_grads.astype(jnp.bfloat16), gate_grad_pre, up_grad_pre


def one_expert(operands):
    inputs, out_grads, gate_matrix, up_matrix, down_matrix = operands
    contract_rows = (((0,), (0,)), ((), ()))
    outputs, gate_pre, up_pre, hidden = expert_forward(inputs, gate_matrix, up_matrix, down_matrix)
    input_grads, gate_grad_pre, up_grad_pre = expert_backward(out_grads, gate_pre, up_pre, gate_matrix, up_matrix, down_matrix)
    gate_part = lax.dot_general(inputs, gate_grad_pre, contract_rows, preferred_element_type=jnp.float32).astype(jnp.bfloat16)
    up_part = lax.dot_general(inputs, up_grad_pre, contract_rows, preferred_element_type=jnp.float32).astype(jnp.bfloat16)
    down_part = lax.dot_general(hidden, out_grads, contract_rows, preferred_element_type=jnp.float32).astype(jnp.bfloat16)
    return outputs, input_grads, gate_part, up_part, down_part


def reference(tokens, routes, route_weights, gate_weight, up_weight, down_weight, cotangent):
    group_arrays = (
        tokens.reshape(N_DP, N_EXPERT, TOK_DEV, LATENT),
        routes.reshape(N_DP, N_EXPERT, TOK_DEV, TOP),
        route_weights.reshape(N_DP, N_EXPERT, TOK_DEV, TOP),
        cotangent.reshape(N_DP, N_EXPERT, TOK_DEV, LATENT),
    )

    def one_group(totals, arrays):
        group_tokens, group_routes, group_weights, group_cotangent = arrays
        kept_mask, slot_index = jax.vmap(lambda route_rows: slot_plan(route_rows, EXPERTS, CAPACITY))(group_routes)
        kept_weights = group_weights * kept_mask.reshape(N_EXPERT, TOK_DEV, TOP).astype(jnp.float32)
        token_rows = jnp.repeat(group_tokens, TOP, axis=1)
        grad_rows = (kept_weights[..., None] * group_cotangent[:, :, None, :].astype(jnp.float32)).astype(jnp.bfloat16)
        grad_rows = grad_rows.reshape(N_EXPERT, TOK_DEV * TOP, LATENT)
        packer = jax.vmap(lambda row_values, positions: pack_rows(row_values, positions, EXPERTS, CAPACITY))
        inbox_tokens = packer(token_rows, slot_index).transpose(1, 0, 2, 3).reshape(EXPERTS, N_EXPERT * CAPACITY, LATENT)
        inbox_grads = packer(grad_rows, slot_index).transpose(1, 0, 2, 3).reshape(EXPERTS, N_EXPERT * CAPACITY, LATENT)
        outputs, input_grads, gate_part, up_part, down_part = lax.map(
            one_expert, (inbox_tokens, inbox_grads, gate_weight, up_weight, down_weight))

        def combine(slot_values):
            per_source = slot_values.reshape(EXPERTS, N_EXPERT, CAPACITY, LATENT).transpose(1, 0, 2, 3)
            gathered = jax.vmap(lambda buffer, positions: unpack_rows(buffer, positions, TOP))(per_source, slot_index)
            return gathered.astype(jnp.float32)

        mixed_latent = jnp.sum(combine(outputs) * kept_weights[..., None], axis=2).astype(jnp.bfloat16)
        latent_grad = jnp.sum(combine(input_grads), axis=2).astype(jnp.bfloat16)
        totals = (totals[0] + gate_part.astype(jnp.float32),
                  totals[1] + up_part.astype(jnp.float32),
                  totals[2] + down_part.astype(jnp.float32))
        return totals, (mixed_latent, latent_grad)

    initial = (jnp.zeros((EXPERTS, LATENT, FFN), jnp.float32),
               jnp.zeros((EXPERTS, LATENT, FFN), jnp.float32),
               jnp.zeros((EXPERTS, FFN, LATENT), jnp.float32))
    totals, (mixed_latent, latent_grad) = lax.scan(one_group, initial, group_arrays)
    return (mixed_latent.reshape(TOKENS, LATENT), latent_grad.reshape(TOKENS, LATENT),
            totals[0], totals[1], totals[2])
```

```python
import jax
import jax.numpy as jnp
from jax import lax
from jax.sharding import PartitionSpec as P


def slot_selector(routes, route_weights, expert, capacity):
    named = routes == expert
    mask = jnp.any(named, axis=2)
    weight = jnp.sum(jnp.where(named, route_weights, 0.0), axis=2)
    counts = mask.astype(jnp.int32)
    rank = jnp.cumsum(counts, axis=1) - counts
    rank = jnp.where(mask, rank, capacity)
    select = rank[:, None, :] == jnp.arange(capacity, dtype=jnp.int32)[None, :, None]
    return select, weight


def shards(tokens, routes, route_weights, gate_weight, up_weight, down_weight, cotangent):
    rows, latent = tokens.shape
    top = routes.shape[1]
    experts = lax.axis_size("expert")
    capacity = rows * top // experts
    me = lax.axis_index("expert")
    gather = lambda v: lax.all_gather(v, "expert", axis=0, tiled=False)
    all_routes = gather(routes)
    all_weights = gather(route_weights)
    all_tokens = gather(tokens)
    all_cots = gather(cotangent)
    gate, up, down = gate_weight[0], up_weight[0], down_weight[0]
    select, weight = slot_selector(all_routes, all_weights, me, capacity)
    sel16 = select.astype(jnp.bfloat16)
    slot_weight = jnp.sum(jnp.where(select, weight[:, None, :], 0.0), axis=2)
    pick = (((2,), (1,)), ((0,), (0,)))
    inputs = lax.dot_general(sel16, all_tokens, pick, preferred_element_type=jnp.float32)
    inputs = inputs.astype(jnp.bfloat16).reshape(-1, latent)
    cot_rows = lax.dot_general(sel16, all_cots, pick, preferred_element_type=jnp.float32)
    out_grads = (cot_rows * slot_weight[:, :, None]).astype(jnp.bfloat16).reshape(-1, latent)

    dot = lambda a, b, d: lax.dot_general(a, b, (d, ((), ())), preferred_element_type=jnp.float32)
    gate_pre = dot(inputs, gate, ((1,), (0,)))
    up_pre = dot(inputs, up, ((1,), (0,)))
    sig = jax.nn.sigmoid(gate_pre)
    hidden = (gate_pre * sig * up_pre).astype(jnp.bfloat16)
    outputs = dot(hidden, down, ((1,), (0,))).astype(jnp.bfloat16)
    hidden_grad = dot(out_grads, down, ((1,), (1,)))
    up_gp = (hidden_grad * gate_pre * sig).astype(jnp.bfloat16)
    gate_gp = (hidden_grad * up_pre * sig * (1.0 + gate_pre * (1.0 - sig))).astype(jnp.bfloat16)
    slot_grad = (dot(gate_gp, gate, ((1,), (1,))) + dot(up_gp, up, ((1,), (1,)))).astype(jnp.bfloat16)

    put = (((1,), (1,)), ((0,), (0,)))
    out_part = lax.dot_general(
        sel16, outputs.reshape(experts, capacity, latent), put, preferred_element_type=jnp.float32
    )
    out_part = (out_part * weight[:, :, None]).astype(jnp.bfloat16)
    grad_part = lax.dot_general(
        sel16, slot_grad.reshape(experts, capacity, latent), put, preferred_element_type=jnp.float32
    ).astype(jnp.bfloat16)
    scatter = lambda v, axis, dim: lax.psum_scatter(v, axis, scatter_dimension=dim, tiled=True)
    mixed = scatter(out_part.reshape(-1, latent), "expert", 0)
    lgrad = scatter(grad_part.reshape(-1, latent), "expert", 0)

    pair = dot(inputs, jnp.concatenate([gate_gp, up_gp], axis=1), ((0,), (0,)))
    pair_share = scatter(pair.astype(jnp.bfloat16), "dp", 0).astype(jnp.float32)
    down_part = dot(out_grads, hidden, ((0,), (0,))).astype(jnp.bfloat16)
    down_share = scatter(down_part, "dp", 0).astype(jnp.float32)
    ffn = hidden.shape[1]
    return (mixed, lgrad, pair_share[:, :ffn][None], pair_share[:, ffn:][None], down_share.T[None])


def solution(mesh):
    rows = P(("dp", "expert"), None)
    per_expert = P("expert", None, None)
    return jax.shard_map(
        shards,
        mesh=mesh,
        in_specs=(rows, rows, rows, per_expert, per_expert, per_expert, rows),
        out_specs=(rows, rows, P("expert", "dp", None), P("expert", "dp", None), P("expert", None, "dp")),
        check_vma=False,
    )
```

```python
import functools
import math

import jax
import jax.numpy as jnp
from jax import lax
from jax.experimental import pallas as pl
from jax.experimental.pallas import tpu as pltpu
from jax.sharding import PartitionSpec as P

F32, BF16 = jnp.float32, jnp.bfloat16


def dot(a, b, contract):
    return lax.dot_general(a, b, (contract, ((), ())), preferred_element_type=F32)


ROWS_COLS = ((1,), (0,))
LAST_LAST = ((1,), (1,))
FIRST_FIRST = ((0,), (0,))


def kernel(
    side, nd, capacity, cap,
    routes_ref, weights_ref, tok_ref, cot_ref, gate_ref, up_ref, down_ref,
    mixed_ref, lgrad_ref, gate_out, up_out, down_out,
    meta, line, stage, inbox, back_stage, back, part, hop, gate_pre, up_pre, hid, gate_gp, up_gp,
    dp_gate, dp_up, dp_down, in_gate, in_up, in_down,
    meta_send, meta_recv, line_send, line_recv, slot_send, slot_recv, back_send, back_recv,
    hop_send, hop_recv, dp_send, dp_recv,
):
    experts = side * side
    top, rows = routes_ref.shape
    latent = tok_ref.shape[1]
    ffn = gate_ref.shape[1]
    share = latent // nd
    slots = side * cap
    me = lax.axis_index("expert")
    dp = lax.axis_index("dp")
    z, p = me // side, me % side

    def at_line(k):
        return {"expert": k * side + p}

    def at_plane(k):
        return {"expert": z * side + k}

    def remote(src, dst, send, recv, device):
        return pltpu.make_async_remote_copy(
            src_ref=src, dst_ref=dst, send_sem=send, recv_sem=recv,
            device_id=device, device_id_type=pl.DeviceIdType.MESH,
        )

    def others(count, mine, body):
        def turn(r, carry):
            body((mine + r) % count)
            return carry
        lax.fori_loop(1, count, turn, 0)

    def loop(count, body):
        def turn(i, carry):
            body(i)
            return carry
        lax.fori_loop(0, count, turn, 0)

    barrier = pltpu.get_barrier_semaphore()

    def greet(device):
        pl.semaphore_signal(barrier, inc=1, device_id=device, device_id_type=pl.DeviceIdType.MESH)

    others(side, z, lambda k: greet(at_line(k)))
    others(side, p, lambda k: greet(at_plane(k)))
    others(nd, dp, lambda k: greet({"dp": k}))

    name = lax.broadcasted_iota(jnp.int32, (experts, rows), 0)
    mask = jnp.zeros((experts, rows), F32)
    weight = jnp.zeros((experts, rows), F32)
    for k in range(top):
        named = routes_ref[k : k + 1, :] == name
        mask = jnp.where(named, 1.0, mask)
        weight = jnp.where(named, weights_ref[k : k + 1, :], weight)
    before = lax.broadcasted_iota(jnp.int32, (rows, rows), 0) < lax.broadcasted_iota(
        jnp.int32, (rows, rows), 1
    )
    rank = dot(mask.astype(BF16), jnp.where(before, 1.0, 0.0).astype(BF16), ROWS_COLS)
    kept = jnp.where(rank < float(capacity), mask, 0.0)
    meta[z, 0:experts, :] = jnp.where(kept > 0.0, rank, -1.0)
    meta[z, experts : 2 * experts, :] = weight
    line[0, z] = tok_ref[...]
    line[1, z] = cot_ref[...]

    pl.semaphore_wait(barrier, 2 * (side - 1) + nd - 1)

    def meta_copy(src, dst):
        return remote(meta.at[src], meta.at[src], meta_send.at[dst], meta_recv.at[src], at_line(dst))

    def line_copy(t, way, block, dst):
        return remote(
            line.at[t, block], line.at[t, block], line_send.at[t, way, block],
            line_recv.at[t, block], at_line(dst),
        )

    def rows_of(block):
        return pl.ds(pl.multiple_of(block * cap, cap), cap)

    def slot_copy(t, src, dst, block):
        return remote(
            stage.at[t, dst, rows_of(block)], inbox.at[t, src, rows_of(block)],
            slot_send.at[t, dst, block], slot_recv.at[t, src, block], at_plane(dst),
        )

    def back_copy(t, src, dst):
        return remote(
            back_stage.at[t, dst], back.at[t, src], back_send.at[t, dst], back_recv.at[t, src],
            at_plane(dst),
        )

    def hop_copy(t, way, block, dst):
        return remote(
            part.at[t, block], hop.at[t, way, block], hop_send.at[t, way, block],
            hop_recv.at[t, way, block], at_line(dst),
        )

    def dp_copy(kind, src, dst):
        out, come = ((dp_gate, in_gate), (dp_up, in_up), (dp_down, in_down))[kind]
        return remote(
            out.at[dst], come.at[src], dp_send.at[kind, dst], dp_recv.at[kind, src], {"dp": dst}
        )

    others(side, z, lambda k: meta_copy(z, k).start())

    slot_name = lax.broadcasted_iota(jnp.int32, (cap, rows), 0).astype(F32)

    def selector(block):
        hot, scaled = [], []
        for q in range(side):
            ranks = meta[block, pl.ds(z * side + q, 1), :]
            scale = meta[block, pl.ds(experts + z * side + q, 1), :]
            hit = slot_name == ranks
            hot.append(jnp.where(hit, 1.0, 0.0))
            scaled.append(jnp.where(hit, scale, 0.0))
        return jnp.concatenate(hot, axis=0), jnp.concatenate(scaled, axis=0)

    def pack(t, block):
        hot, scaled = selector(block)
        picked = dot(hot.astype(BF16), line[t, block], ROWS_COLS)
        if t == 1:
            picked = picked * jnp.sum(scaled, axis=1, keepdims=True)
        picked = picked.astype(BF16)
        for q in range(side):
            stage[t, q, rows_of(block), :] = picked[q * cap : (q + 1) * cap]
        others(side, p, lambda q: slot_copy(t, p, q, block).start())
        inbox[t, p, rows_of(block), :] = stage[t, p, rows_of(block), :]

    def arrive(t, d):
        def come(block):
            @pl.when(d > 0)
            def _():
                if t == 0:
                    meta_copy(block, z).wait_recv()
                line_copy(t, 0, block, z).wait_recv()

        @pl.when(z - d >= 0)
        def _():
            come(z - d)

            @pl.when(z + 1 < side)
            def _():
                line_copy(t, 0, z - d, z + 1).start()

        @pl.when(z + d < side)
        def _():
            come(z + d)

            @pl.when(z > 0)
            def _():
                line_copy(t, 1, z + d, z - 1).start()

        @pl.when(z - d >= 0)
        def _():
            pack(t, z - d)

        @pl.when((d > 0) & (z + d < side))
        def _():
            pack(t, z + d)

    def slots_in(t, src):
        @pl.when(src != p)
        def _():
            loop(side, lambda block: slot_copy(t, src, p, block).wait_recv())

    def hand_back(t, dst, value):
        back_stage[t, dst] = value

        @pl.when(dst != p)
        def _():
            back_copy(t, p, dst).start()

        @pl.when(dst == p)
        def _():
            back[t, p] = back_stage[t, p]

    def forward(src):
        slots_in(0, src)
        inputs = inbox[0, src]
        pre = dot(inputs, gate_ref[...], ROWS_COLS)
        raised = dot(inputs, up_ref[...], ROWS_COLS)
        gate_pre[src] = pre
        up_pre[src] = raised
        hidden = (pre * jax.nn.sigmoid(pre) * raised).astype(BF16)
        hid[src] = hidden
        hand_back(0, src, dot(hidden, down_ref[...], ROWS_COLS).astype(BF16))

    def backward(src):
        pre, raised = gate_pre[src], up_pre[src]
        sig = jax.nn.sigmoid(pre)
        hidden_grad = dot(inbox[1, src], down_ref[...], LAST_LAST)
        up_g = (hidden_grad * pre * sig).astype(BF16)
        gate_g = (hidden_grad * raised * sig * (1.0 + pre * (1.0 - sig))).astype(BF16)
        up_gp[src] = up_g
        gate_gp[src] = gate_g
        slot_grad = dot(gate_g, gate_ref[...], LAST_LAST) + dot(up_g, up_ref[...], LAST_LAST)
        hand_back(1, src, slot_grad.astype(BF16))

    loop(side, lambda d: arrive(0, d))

    def cot_and_forward(d):
        arrive(1, d)
        forward((p + d) % side)

    loop(side, cot_and_forward)

    def columns(j):
        return pl.ds(pl.multiple_of(j * share, share), share)

    def flat(ref, width):
        return ref.reshape(side * slots, width)

    def weight_part(kind, j):
        if kind == 2:
            grads = flat(inbox[1, :, :, columns(j)], share)
            return dot(flat(hid[...], ffn), grads, FIRST_FIRST).astype(BF16)
        grads = flat((gate_gp if kind == 0 else up_gp)[...], ffn)
        return dot(flat(inbox[0, :, :, columns(j)], share), grads, FIRST_FIRST).astype(BF16)

    def share_out(kind):
        def one(j):
            (dp_gate, dp_up, dp_down)[kind][j] = weight_part(kind, j)
            dp_copy(kind, dp, j).start()
        others(nd, dp, one)

    others(side, p, lambda src: slots_in(1, src))
    share_out(2)
    loop(side, lambda r: backward((p + r) % side))
    share_out(0)
    share_out(1)

    def combine(t, block):
        hot, scaled = selector(block)
        values = back[t, :, rows_of(block), :].reshape(side * cap, latent)
        if t == 1:
            return dot(hot.astype(BF16), values, FIRST_FIRST)
        high = scaled.astype(BF16)
        low = (scaled - high.astype(F32)).astype(BF16)
        return dot(high, values, FIRST_FIRST) + dot(low, values, FIRST_FIRST)

    def pass_on(t, way, block, dst, has_prior):
        total = combine(t, block)
        part[t, block] = total.astype(BF16)

        @pl.when(has_prior)
        def _():
            hop_copy(t, way, block, z).wait_recv()
            part[t, block] = (part[t, block].astype(F32) + hop[t, way, block].astype(F32)).astype(BF16)

        hop_copy(t, way, block, dst).start()

    def reduce_line(t):
        others(side, p, lambda src: back_copy(t, src, p).wait_recv())

        def step(i):
            @pl.when(side - 1 - i > z)
            def _():
                pass_on(t, 0, side - 1 - i, z + 1, z > 0)

            @pl.when(i < z)
            def _():
                pass_on(t, 1, i, z - 1, z + 1 < side)

        loop(side - 1, step)

    def finish(t, out):
        out[...] = combine(t, z).astype(BF16)

        def add(way):
            hop_copy(t, way, z, z).wait_recv()
            out[...] = (out[...].astype(F32) + hop[t, way, z].astype(F32)).astype(BF16)

        @pl.when(z > 0)
        def _():
            add(0)

        @pl.when(z + 1 < side)
        def _():
            add(1)

    reduce_line(0)
    reduce_line(1)
    finish(0, mixed_ref)
    for kind, out in ((2, down_out), (0, gate_out), (1, up_out)):
        out[0] = weight_part(kind, dp).astype(F32)
    finish(1, lgrad_ref)
    for kind, out, come in ((2, down_out, in_down), (0, gate_out, in_gate), (1, up_out, in_up)):
        def add_share(j):
            dp_copy(kind, j, dp).wait_recv()
            out[0] = out[0] + come[j].astype(F32)
        others(nd, dp, add_share)

    others(side, z, lambda k: meta_copy(z, k).wait_send())
    for t in range(2):
        def line_sent(block):
            @pl.when((block <= z) & (z + 1 < side))
            def _():
                line_copy(t, 0, block, z + 1).wait_send()

            @pl.when((block >= z) & (z > 0))
            def _():
                line_copy(t, 1, block, z - 1).wait_send()

            @pl.when(block > z)
            def _():
                hop_copy(t, 0, block, z + 1).wait_send()

            @pl.when(block < z)
            def _():
                hop_copy(t, 1, block, z - 1).wait_send()

        loop(side, line_sent)

        def plane_sent(q):
            loop(side, lambda block: slot_copy(t, p, q, block).wait_send())
            back_copy(t, p, q).wait_send()

        others(side, p, plane_sent)
    for kind in range(3):
        others(nd, dp, lambda j: dp_copy(kind, dp, j).wait_send())


def shards(tokens, routes, route_weights, gate_weight, up_weight, down_weight, cotangent):
    rows, latent = tokens.shape
    top = routes.shape[1]
    ffn = gate_weight.shape[2]
    experts, nd = lax.axis_size("expert"), lax.axis_size("dp")
    side = math.isqrt(experts)
    assert side * side == experts
    capacity = rows * top // experts
    cap = -(-capacity // 16) * 16
    slots, share = side * cap, latent // nd
    vmem = pl.BlockSpec(memory_space=pltpu.VMEM)
    dma = lambda *shape: pltpu.SemaphoreType.DMA(shape)
    return pl.pallas_call(
        functools.partial(kernel, side, nd, capacity, cap),
        out_shape=(
            jax.ShapeDtypeStruct((rows, latent), BF16),
            jax.ShapeDtypeStruct((rows, latent), BF16),
            jax.ShapeDtypeStruct((1, share, ffn), F32),
            jax.ShapeDtypeStruct((1, share, ffn), F32),
            jax.ShapeDtypeStruct((1, ffn, share), F32),
        ),
        in_specs=[vmem] * 7,
        out_specs=[vmem] * 5,
        scratch_shapes=[
            pltpu.VMEM((side, 2 * experts, rows), F32),
            pltpu.VMEM((2, side, rows, latent), BF16),
            pltpu.VMEM((2, side, slots, latent), BF16),
            pltpu.VMEM((2, side, slots, latent), BF16),
            pltpu.VMEM((2, side, slots, latent), BF16),
            pltpu.VMEM((2, side, slots, latent), BF16),
            pltpu.VMEM((2, side, rows, latent), BF16),
            pltpu.VMEM((2, 2, side, rows, latent), BF16),
            pltpu.VMEM((side, slots, ffn), F32),
            pltpu.VMEM((side, slots, ffn), F32),
            pltpu.VMEM((side, slots, ffn), BF16),
            pltpu.VMEM((side, slots, ffn), BF16),
            pltpu.VMEM((side, slots, ffn), BF16),
            pltpu.VMEM((nd, share, ffn), BF16),
            pltpu.VMEM((nd, share, ffn), BF16),
            pltpu.VMEM((nd, ffn, share), BF16),
            pltpu.VMEM((nd, share, ffn), BF16),
            pltpu.VMEM((nd, share, ffn), BF16),
            pltpu.VMEM((nd, ffn, share), BF16),
            dma(side), dma(side),
            dma(2, 2, side), dma(2, side),
            dma(2, side, side), dma(2, side, side),
            dma(2, side), dma(2, side),
            dma(2, 2, side), dma(2, 2, side),
            dma(3, nd), dma(3, nd),
        ],
        compiler_params=pltpu.CompilerParams(
            collective_id=0, has_side_effects=True, vmem_limit_bytes=60 * 1024 * 1024
        ),
    )(
        routes.T, route_weights.T, tokens, cotangent, gate_weight[0], up_weight[0], down_weight[0]
    )


def solution(mesh):
    rows = P(("dp", "expert"), None)
    per_expert = P("expert", None, None)
    return jax.shard_map(
        shards,
        mesh=mesh,
        in_specs=(rows, rows, rows, per_expert, per_expert, per_expert, rows),
        out_specs=(
            rows, rows, P("expert", "dp", None), P("expert", "dp", None), P("expert", None, "dp")
        ),
        check_vma=False,
    )
```

```python
import functools
import math

import jax
import jax.numpy as jnp
from jax import lax
from jax.experimental import pallas as pl
from jax.experimental.pallas import tpu as pltpu
from jax.sharding import PartitionSpec as P

F32, BF16 = jnp.float32, jnp.bfloat16


def dot(a, b, contract):
    return lax.dot_general(a, b, (contract, ((), ())), preferred_element_type=F32)


ROWS_COLS = ((1,), (0,))
LAST_LAST = ((1,), (1,))
FIRST_FIRST = ((0,), (0,))


def kernel(
    side, nd, capacity, cap,
    routes_ref, weights_ref, tok_hbm, cot_hbm, gate_hbm, up_hbm, down_hbm,
    mixed_ref, lgrad_ref, gate_parts, up_parts, down_parts,
    gate_ref, up_ref, down_ref,
    meta, line, stage, inbox, back_stage, back, part, hop, gate_pre, up_pre, hid, gate_gp, up_gp,
    dp_gate, dp_up, dp_down,
    load_sem, meta_send, meta_recv, line_send, line_recv, slot_send, slot_recv, back_send,
    back_recv, hop_send, hop_recv, dp_send, dp_recv,
):
    experts = side * side
    top, rows = routes_ref.shape
    latent, ffn = gate_ref.shape
    share = latent // nd
    width = side * cap
    me = lax.axis_index("expert")
    dp = lax.axis_index("dp")
    z, p = me // side, me % side

    def at_line(k):
        return {"expert": k * side + p}

    def at_plane(k):
        return {"expert": z * side + k}

    def remote(src, dst, send, recv, device):
        return pltpu.make_async_remote_copy(
            src_ref=src, dst_ref=dst, send_sem=send, recv_sem=recv,
            device_id=device, device_id_type=pl.DeviceIdType.MESH,
        )

    def loop(first, last, body):
        def turn(i, carry):
            body(i)
            return carry
        lax.fori_loop(first, last, turn, 0)

    def others(count, mine, body):
        loop(1, count, lambda r: body((mine + r) % count))

    loads = [
        pltpu.make_async_copy(src, dst, load_sem.at[i])
        for i, (src, dst) in enumerate((
            (tok_hbm, line.at[0, z]), (cot_hbm, line.at[1, z]),
            (gate_hbm, gate_ref), (up_hbm, up_ref), (down_hbm, down_ref),
        ))
    ]
    for load in loads:
        load.start()

    barrier = pltpu.get_barrier_semaphore()

    def greet(device):
        pl.semaphore_signal(barrier, inc=1, device_id=device, device_id_type=pl.DeviceIdType.MESH)

    others(side, z, lambda k: greet(at_line(k)))
    others(side, p, lambda k: greet(at_plane(k)))
    others(nd, dp, lambda k: greet({"dp": k}))

    name = lax.broadcasted_iota(jnp.int32, (experts, rows), 0)
    mask = jnp.zeros((experts, rows), F32)
    weight = jnp.zeros((experts, rows), F32)
    for k in range(top):
        named = routes_ref[k : k + 1, :] == name
        mask = jnp.where(named, 1.0, mask)
        weight = jnp.where(named, weights_ref[k : k + 1, :], weight)
    before = lax.broadcasted_iota(jnp.int32, (rows, rows), 0) < lax.broadcasted_iota(
        jnp.int32, (rows, rows), 1
    )
    rank = dot(mask.astype(BF16), jnp.where(before, 1.0, 0.0).astype(BF16), ROWS_COLS)
    kept = jnp.where(rank < float(capacity), mask, 0.0)
    meta[z, 0:experts, :] = jnp.where(kept > 0.0, rank, -1.0)
    meta[z, experts : 2 * experts, :] = weight
    loads[0].wait()
    pl.semaphore_wait(barrier, 2 * (side - 1) + nd - 1)

    def meta_copy(src, dst):
        return remote(meta.at[src], meta.at[src], meta_send.at[dst], meta_recv.at[src], at_line(dst))

    def line_copy(t, way, block, dst):
        return remote(
            line.at[t, block], line.at[t, block], line_send.at[t, way, block],
            line_recv.at[t, block], at_line(dst),
        )

    def slot_copy(t, block, src, dst):
        return remote(
            stage.at[t, block, dst], inbox.at[t, block, src],
            slot_send.at[t, block, dst], slot_recv.at[t, block, src], at_plane(dst),
        )

    def back_copy(t, block, src, dst):
        return remote(
            back_stage.at[t, block, dst], back.at[t, block, src],
            back_send.at[t, block, dst], back_recv.at[t, block, src], at_plane(dst),
        )

    def hop_copy(t, way, block, dst):
        return remote(
            part.at[t, block], hop.at[t, way, block], hop_send.at[t, way, block],
            hop_recv.at[t, way, block], at_line(dst),
        )

    def dp_copy(kind, src, dst):
        out, come = ((dp_gate, gate_parts), (dp_up, up_parts), (dp_down, down_parts))[kind]
        return remote(
            out.at[dst], come.at[src], dp_send.at[kind, dst], dp_recv.at[kind, src], {"dp": dst}
        )

    def own_share(kind):
        out, come = ((dp_gate, gate_parts), (dp_up, up_parts), (dp_down, down_parts))[kind]
        return pltpu.make_async_copy(out.at[dp], come.at[dp], dp_send.at[kind, dp])

    slot_name = lax.broadcasted_iota(jnp.int32, (cap, rows), 0).astype(F32)

    def selector(block):
        hot, scaled = [], []
        for q in range(side):
            ranks = meta[block, pl.ds(z * side + q, 1), :]
            scale = meta[block, pl.ds(experts + z * side + q, 1), :]
            hit = slot_name == ranks
            hot.append(jnp.where(hit, 1.0, 0.0))
            scaled.append(jnp.where(hit, scale, 0.0))
        return jnp.concatenate(hot, axis=0), jnp.concatenate(scaled, axis=0)

    def visit(d, body):
        def one(s):
            block = z - d + 2 * d * s

            @pl.when((block >= 0) & (block < side) & (d + 1 > s))
            def _():
                body(block)
        loop(0, 2, one)

    def pack(t, block):
        hot, scaled = selector(block)
        picked = dot(hot.astype(BF16), line[t, block], ROWS_COLS)
        if t == 1:
            picked = picked * jnp.sum(scaled, axis=1, keepdims=True)
        stage[t, block] = picked.astype(BF16).reshape(side, cap, latent)
        others(side, p, lambda q: slot_copy(t, block, p, q).start())
        inbox[t, block, p] = stage[t, block, p]

    def arrive(t, d):
        def come(block):
            @pl.when(d > 0)
            def _():
                if t == 0:
                    meta_copy(block, z).wait_recv()
                line_copy(t, 0, block, z).wait_recv()

        @pl.when(z - d >= 0)
        def _():
            come(z - d)

            @pl.when(z + 1 < side)
            def _():
                line_copy(t, 0, z - d, z + 1).start()

        @pl.when(z + d < side)
        def _():
            come(z + d)

            @pl.when(z > 0)
            def _():
                line_copy(t, 1, z + d, z - 1).start()

        if t == 0:
            @pl.when(d == 0)
            def _():
                others(side, z, lambda k: meta_copy(z, k).start())
        visit(d, lambda block: pack(t, block))

    def hand_back(t, block, value):
        back_stage[t, block] = value.astype(BF16).reshape(side, cap, latent)
        others(side, p, lambda q: back_copy(t, block, p, q).start())
        back[t, block, p] = back_stage[t, block, p]

    def slots_in(t, block):
        others(side, p, lambda q: slot_copy(t, block, q, p).wait_recv())

    def forward(block):
        slots_in(0, block)
        inputs = inbox[0, block].reshape(width, latent)
        pre = dot(inputs, gate_ref[...], ROWS_COLS)
        raised = dot(inputs, up_ref[...], ROWS_COLS)
        gate_pre[block] = pre
        up_pre[block] = raised
        hidden = (pre * jax.nn.sigmoid(pre) * raised).astype(BF16)
        hid[block] = hidden
        hand_back(0, block, dot(hidden, down_ref[...], ROWS_COLS))

    def backward(block):
        pre, raised = gate_pre[block], up_pre[block]
        sig = jax.nn.sigmoid(pre)
        grads = inbox[1, block].reshape(width, latent)
        hidden_grad = dot(grads, down_ref[...], LAST_LAST)
        up_g = (hidden_grad * pre * sig).astype(BF16)
        gate_g = (hidden_grad * raised * sig * (1.0 + pre * (1.0 - sig))).astype(BF16)
        up_gp[block] = up_g
        gate_gp[block] = gate_g
        hand_back(
            1, block, dot(gate_g, gate_ref[...], LAST_LAST) + dot(up_g, up_ref[...], LAST_LAST)
        )

    def columns(j):
        return pl.ds(pl.multiple_of(j * share, share), share)

    def weight_part(kind, j):
        flat = lambda value: value.reshape(side * width, value.shape[-1])
        if kind == 2:
            return dot(flat(hid[...]), flat(inbox[1, :, :, :, columns(j)]), FIRST_FIRST).astype(BF16)
        grads = flat((gate_gp if kind == 0 else up_gp)[...])
        return dot(flat(inbox[0, :, :, :, columns(j)]), grads, FIRST_FIRST).astype(BF16)

    def share_out(kind):
        def one(j):
            (dp_gate, dp_up, dp_down)[kind][j] = weight_part(kind, j)
            dp_copy(kind, dp, j).start()
        others(nd, dp, one)

    def keep_own(kind):
        (dp_gate, dp_up, dp_down)[kind][dp] = weight_part(kind, dp)
        own_share(kind).start()

    def combine(t, block):
        others(side, p, lambda q: back_copy(t, block, q, p).wait_recv())
        hot, scaled = selector(block)
        values = back[t, block].reshape(width, latent)
        if t == 1:
            return dot(hot.astype(BF16), values, FIRST_FIRST)
        high = scaled.astype(BF16)
        low = (scaled - high.astype(F32)).astype(BF16)
        return dot(high, values, FIRST_FIRST) + dot(low, values, FIRST_FIRST)

    def pass_on(t, way, block, dst, has_prior):
        total = combine(t, block)

        @pl.when(has_prior)
        def _():
            hop_copy(t, way, block, z).wait_recv()
            part[t, block] = (total + hop[t, way, block].astype(F32)).astype(BF16)

        @pl.when(jnp.logical_not(has_prior))
        def _():
            part[t, block] = total.astype(BF16)

        hop_copy(t, way, block, dst).start()

    def wave(t, w):
        @pl.when(w >= z)
        def _():
            pass_on(t, 0, side - 1 - (w - z), z + 1, z > 0)

        @pl.when(w >= side - 1 - z)
        def _():
            pass_on(t, 1, w - (side - 1 - z), z - 1, z + 1 < side)

    def finish(t, out):
        out[...] = combine(t, z).astype(BF16)

        def add(way):
            hop_copy(t, way, z, z).wait_recv()
            out[...] = (out[...].astype(F32) + hop[t, way, z].astype(F32)).astype(BF16)

        @pl.when(z > 0)
        def _():
            add(0)

        @pl.when(z + 1 < side)
        def _():
            add(1)

    def token_step(d):
        arrive(0, d)

        @pl.when(d > 0)
        def _():
            @pl.when(d == 1)
            def _():
                for load in loads[2:]:
                    load.wait()
            visit(d - 1, forward)

    def grad_step(d):
        arrive(1, d)

        @pl.when(d == 0)
        def _():
            visit(side - 1, forward)

        @pl.when(d > 0)
        def _():
            visit(d - 1, lambda block: slots_in(1, block))
            visit(d - 1, backward)
            wave(0, d - 1)

    loop(0, side, token_step)
    loads[1].wait()
    loop(0, side, grad_step)
    visit(side - 1, lambda block: slots_in(1, block))
    visit(side - 1, backward)
    share_out(0)
    share_out(1)
    share_out(2)
    wave(1, 0)
    finish(0, mixed_ref)
    for w in range(1, side - 1):
        wave(1, w)
        if w <= 3:
            keep_own(w - 1)
    for kind in range(max(0, min(side - 2, 3)), 3):
        keep_own(kind)
    finish(1, lgrad_ref)

    for kind in range(3):
        others(nd, dp, lambda j: dp_copy(kind, j, dp).wait_recv())
        own_share(kind).wait()
        others(nd, dp, lambda j: dp_copy(kind, dp, j).wait_send())
    others(side, z, lambda k: meta_copy(z, k).wait_send())
    for t in range(2):
        def line_sent(block):
            @pl.when((block <= z) & (z + 1 < side))
            def _():
                line_copy(t, 0, block, z + 1).wait_send()

            @pl.when((block >= z) & (z > 0))
            def _():
                line_copy(t, 1, block, z - 1).wait_send()

            @pl.when(block > z)
            def _():
                hop_copy(t, 0, block, z + 1).wait_send()

            @pl.when(block < z)
            def _():
                hop_copy(t, 1, block, z - 1).wait_send()

            def plane_sent(q):
                slot_copy(t, block, p, q).wait_send()
                back_copy(t, block, p, q).wait_send()

            others(side, p, plane_sent)

        loop(0, side, line_sent)


def add_parts(mixed_ref, lgrad_ref, gate_parts, up_parts, down_parts, *outs):
    outs[0][...] = mixed_ref[...]
    outs[1][...] = lgrad_ref[...]
    for parts, out in zip((gate_parts, up_parts, down_parts), outs[2:]):
        out[0] = jnp.sum(parts[...].astype(F32), axis=0)


def shards(tokens, routes, route_weights, gate_weight, up_weight, down_weight, cotangent):
    rows, latent = tokens.shape
    top = routes.shape[1]
    ffn = gate_weight.shape[2]
    experts, nd = lax.axis_size("expert"), lax.axis_size("dp")
    side = math.isqrt(experts)
    assert side * side == experts
    capacity = rows * top // experts
    cap = -(-capacity // 16) * 16
    width, share = side * cap, latent // nd
    vmem = pl.BlockSpec(memory_space=pltpu.VMEM)
    hbm = pl.BlockSpec(memory_space=pl.ANY)
    dma = lambda *shape: pltpu.SemaphoreType.DMA(shape)
    row_out = jax.ShapeDtypeStruct((rows, latent), BF16)
    params = functools.partial(pltpu.CompilerParams, vmem_limit_bytes=60 * 1024 * 1024)
    parts = pl.pallas_call(
        functools.partial(kernel, side, nd, capacity, cap),
        out_shape=(
            row_out,
            row_out,
            jax.ShapeDtypeStruct((nd, share, ffn), BF16),
            jax.ShapeDtypeStruct((nd, share, ffn), BF16),
            jax.ShapeDtypeStruct((nd, ffn, share), BF16),
        ),
        in_specs=[vmem] * 2 + [hbm] * 5,
        out_specs=[vmem] * 2 + [hbm] * 3,
        scratch_shapes=[
            pltpu.VMEM((latent, ffn), BF16),
            pltpu.VMEM((latent, ffn), BF16),
            pltpu.VMEM((ffn, latent), BF16),
            pltpu.VMEM((side, 2 * experts, rows), F32),
            pltpu.VMEM((2, side, rows, latent), BF16),
            pltpu.VMEM((2, side, side, cap, latent), BF16),
            pltpu.VMEM((2, side, side, cap, latent), BF16),
            pltpu.VMEM((2, side, side, cap, latent), BF16),
            pltpu.VMEM((2, side, side, cap, latent), BF16),
            pltpu.VMEM((2, side, rows, latent), BF16),
            pltpu.VMEM((2, 2, side, rows, latent), BF16),
            pltpu.VMEM((side, width, ffn), F32),
            pltpu.VMEM((side, width, ffn), F32),
            pltpu.VMEM((side, width, ffn), BF16),
            pltpu.VMEM((side, width, ffn), BF16),
            pltpu.VMEM((side, width, ffn), BF16),
            pltpu.VMEM((nd, share, ffn), BF16),
            pltpu.VMEM((nd, share, ffn), BF16),
            pltpu.VMEM((nd, ffn, share), BF16),
            dma(5), dma(side), dma(side),
            dma(2, 2, side), dma(2, side),
            dma(2, side, side), dma(2, side, side),
            dma(2, side, side), dma(2, side, side),
            dma(2, 2, side), dma(2, 2, side),
            dma(3, nd), dma(3, nd),
        ],
        compiler_params=params(collective_id=0, has_side_effects=True),
    )(
        routes.T, route_weights.T, tokens, cotangent, gate_weight[0], up_weight[0], down_weight[0]
    )
    return pl.pallas_call(
        add_parts,
        out_shape=(
            row_out,
            row_out,
            jax.ShapeDtypeStruct((1, share, ffn), F32),
            jax.ShapeDtypeStruct((1, share, ffn), F32),
            jax.ShapeDtypeStruct((1, ffn, share), F32),
        ),
        in_specs=[vmem] * 5,
        out_specs=[vmem] * 5,
        compiler_params=params(),
    )(*parts)


def solution(mesh):
    rows = P(("dp", "expert"), None)
    per_expert = P("expert", None, None)
    return jax.shard_map(
        shards,
        mesh=mesh,
        in_specs=(rows, rows, rows, per_expert, per_expert, per_expert, rows),
        out_specs=(
            rows, rows, P("expert", "dp", None), P("expert", "dp", None), P("expert", None, "dp")
        ),
        check_vma=False,
    )
```

```python
import functools
import math

import jax
import jax.numpy as jnp
from jax import lax
from jax.experimental import pallas as pl
from jax.experimental.pallas import tpu as pltpu
from jax.sharding import PartitionSpec as P

F32, BF16 = jnp.float32, jnp.bfloat16


def dot(a, b, contract):
    return lax.dot_general(a, b, (contract, ((), ())), preferred_element_type=F32)


ROWS_COLS = ((1,), (0,))
LAST_LAST = ((1,), (1,))
FIRST_FIRST = ((0,), (0,))


def kernel(
    side, nd, capacity, cap,
    routes_ref, weights_ref, tok_hbm, cot_hbm, gate_hbm, up_hbm, down_hbm,
    mixed_ref, lgrad_ref, gate_parts, up_parts, down_parts,
    gate_ref, up_ref, down_ref,
    meta, line, stage, inbox, back_stage, back, part, home, total, gate_pre, up_pre, hid, gate_gp, up_gp,
    dp_gate, dp_up, dp_down,
    load_sem, meta_send, meta_recv, line_send, line_recv, slot_send, slot_recv, back_send,
    back_recv, home_send, home_recv, dp_send, dp_recv,
):
    experts = side * side
    top, rows = routes_ref.shape
    latent, ffn = gate_ref.shape
    share = latent // nd
    width = side * cap
    me = lax.axis_index("expert")
    dp = lax.axis_index("dp")
    z, p = me // side, me % side

    def at_line(k):
        return {"expert": k * side + p}

    def at_plane(k):
        return {"expert": z * side + k}

    def remote(src, dst, send, recv, device):
        return pltpu.make_async_remote_copy(
            src_ref=src, dst_ref=dst, send_sem=send, recv_sem=recv,
            device_id=device, device_id_type=pl.DeviceIdType.MESH,
        )

    def loop(first, last, body):
        def turn(i, carry):
            body(i)
            return carry
        lax.fori_loop(first, last, turn, 0)

    def others(count, mine, body):
        loop(1, count, lambda r: body((mine + r) % count))

    loads = [
        pltpu.make_async_copy(src, dst, load_sem.at[i])
        for i, (src, dst) in enumerate((
            (tok_hbm, line.at[0, z]), (cot_hbm, line.at[1, z]),
            (gate_hbm, gate_ref), (up_hbm, up_ref), (down_hbm, down_ref),
        ))
    ]
    for load in loads:
        load.start()

    barrier = pltpu.get_barrier_semaphore()

    def greet(device):
        pl.semaphore_signal(barrier, inc=1, device_id=device, device_id_type=pl.DeviceIdType.MESH)

    others(side, z, lambda k: greet(at_line(k)))
    others(side, p, lambda k: greet(at_plane(k)))
    others(nd, dp, lambda k: greet({"dp": k}))

    name = lax.broadcasted_iota(jnp.int32, (experts, rows), 0)
    mask = jnp.zeros((experts, rows), F32)
    weight = jnp.zeros((experts, rows), F32)
    for k in range(top):
        named = routes_ref[k : k + 1, :] == name
        mask = jnp.where(named, 1.0, mask)
        weight = jnp.where(named, weights_ref[k : k + 1, :], weight)
    before = lax.broadcasted_iota(jnp.int32, (rows, rows), 0) < lax.broadcasted_iota(
        jnp.int32, (rows, rows), 1
    )
    rank = dot(mask.astype(BF16), jnp.where(before, 1.0, 0.0).astype(BF16), ROWS_COLS)
    kept = jnp.where(rank < float(capacity), mask, 0.0)
    meta[z, 0:experts, :] = jnp.where(kept > 0.0, rank, -1.0)
    meta[z, experts : 2 * experts, :] = weight
    loads[0].wait()
    pl.semaphore_wait(barrier, 2 * (side - 1) + nd - 1)

    def meta_copy(src, dst):
        return remote(meta.at[src], meta.at[src], meta_send.at[dst], meta_recv.at[src], at_line(dst))

    def line_copy(t, way, block, dst):
        return remote(
            line.at[t, block], line.at[t, block], line_send.at[t, way, block],
            line_recv.at[t, block], at_line(dst),
        )

    def slot_copy(t, block, src, dst):
        return remote(
            stage.at[t, block, dst], inbox.at[t, block, src],
            slot_send.at[t, block, dst], slot_recv.at[t, block, src], at_plane(dst),
        )

    def back_copy(t, block, src, dst):
        return remote(
            back_stage.at[t, block, dst], back.at[t, block, src],
            back_send.at[t, block, dst], back_recv.at[t, block, src], at_plane(dst),
        )

    def home_copy(t, src, dst):
        return remote(
            part.at[t, dst], home.at[t, src], home_send.at[t, dst], home_recv.at[t, src],
            at_line(dst),
        )

    def dp_copy(kind, src, dst):
        out, come = ((dp_gate, gate_parts), (dp_up, up_parts), (dp_down, down_parts))[kind]
        return remote(
            out.at[dst], come.at[src], dp_send.at[kind, dst], dp_recv.at[kind, src], {"dp": dst}
        )

    def own_share(kind):
        out, come = ((dp_gate, gate_parts), (dp_up, up_parts), (dp_down, down_parts))[kind]
        return pltpu.make_async_copy(out.at[dp], come.at[dp], dp_send.at[kind, dp])

    slot_name = lax.broadcasted_iota(jnp.int32, (cap, rows), 0).astype(F32)

    def selector(block):
        hot, scaled = [], []
        for q in range(side):
            ranks = meta[block, pl.ds(z * side + q, 1), :]
            scale = meta[block, pl.ds(experts + z * side + q, 1), :]
            hit = slot_name == ranks
            hot.append(jnp.where(hit, 1.0, 0.0))
            scaled.append(jnp.where(hit, scale, 0.0))
        return jnp.concatenate(hot, axis=0), jnp.concatenate(scaled, axis=0)

    def visit(d, body):
        def one(s):
            block = z - d + 2 * d * s

            @pl.when((block >= 0) & (block < side) & (d + 1 > s))
            def _():
                body(block)
        loop(0, 2, one)

    def pack(t, block):
        hot, scaled = selector(block)
        picked = dot(hot.astype(BF16), line[t, block], ROWS_COLS)
        if t == 1:
            picked = picked * jnp.sum(scaled, axis=1, keepdims=True)
        stage[t, block] = picked.astype(BF16).reshape(side, cap, latent)
        others(side, p, lambda q: slot_copy(t, block, p, q).start())
        inbox[t, block, p] = stage[t, block, p]

    def arrive(t, d):
        def come(block):
            @pl.when(d > 0)
            def _():
                if t == 0:
                    meta_copy(block, z).wait_recv()
                line_copy(t, 0, block, z).wait_recv()

        @pl.when(z - d >= 0)
        def _():
            come(z - d)

            @pl.when(z + 1 < side)
            def _():
                line_copy(t, 0, z - d, z + 1).start()

        @pl.when(z + d < side)
        def _():
            come(z + d)

            @pl.when(z > 0)
            def _():
                line_copy(t, 1, z + d, z - 1).start()

        if t == 0:
            @pl.when(d == 0)
            def _():
                others(side, z, lambda k: meta_copy(z, k).start())
        visit(d, lambda block: pack(t, block))

    def hand_back(t, block, value):
        back_stage[t, block] = value.astype(BF16).reshape(side, cap, latent)
        others(side, p, lambda q: back_copy(t, block, p, q).start())
        back[t, block, p] = back_stage[t, block, p]

    def slots_in(t, block):
        others(side, p, lambda q: slot_copy(t, block, q, p).wait_recv())

    def forward(block):
        slots_in(0, block)
        inputs = inbox[0, block].reshape(width, latent)
        pre = dot(inputs, gate_ref[...], ROWS_COLS)
        raised = dot(inputs, up_ref[...], ROWS_COLS)
        gate_pre[block] = pre
        up_pre[block] = raised
        hidden = (pre * jax.nn.sigmoid(pre) * raised).astype(BF16)
        hid[block] = hidden
        hand_back(0, block, dot(hidden, down_ref[...], ROWS_COLS))

    def backward(block):
        pre, raised = gate_pre[block], up_pre[block]
        sig = jax.nn.sigmoid(pre)
        grads = inbox[1, block].reshape(width, latent)
        hidden_grad = dot(grads, down_ref[...], LAST_LAST)
        up_g = (hidden_grad * pre * sig).astype(BF16)
        gate_g = (hidden_grad * raised * sig * (1.0 + pre * (1.0 - sig))).astype(BF16)
        up_gp[block] = up_g
        gate_gp[block] = gate_g
        hand_back(
            1, block, dot(gate_g, gate_ref[...], LAST_LAST) + dot(up_g, up_ref[...], LAST_LAST)
        )

    def columns(j):
        return pl.ds(pl.multiple_of(j * share, share), share)

    def weight_part(kind, j):
        flat = lambda value: value.reshape(side * width, value.shape[-1])
        if kind == 2:
            return dot(flat(hid[...]), flat(inbox[1, :, :, :, columns(j)]), FIRST_FIRST).astype(BF16)
        grads = flat((gate_gp if kind == 0 else up_gp)[...])
        return dot(flat(inbox[0, :, :, :, columns(j)]), grads, FIRST_FIRST).astype(BF16)

    def share_out(kind):
        def one(j):
            (dp_gate, dp_up, dp_down)[kind][j] = weight_part(kind, j)
            dp_copy(kind, dp, j).start()
        others(nd, dp, one)

    def keep_own(kind):
        (dp_gate, dp_up, dp_down)[kind][dp] = weight_part(kind, dp)
        own_share(kind).start()

    def combine(t, block):
        others(side, p, lambda q: back_copy(t, block, q, p).wait_recv())
        hot, scaled = selector(block)
        values = back[t, block].reshape(width, latent)
        if t == 1:
            return dot(hot.astype(BF16), values, FIRST_FIRST)
        high = scaled.astype(BF16)
        low = (scaled - high.astype(F32)).astype(BF16)
        return dot(high, values, FIRST_FIRST) + dot(low, values, FIRST_FIRST)

    def deliver(t, d):
        def one(block):
            part[t, block] = combine(t, block).astype(BF16)
            home_copy(t, z, block).start()
        visit(d, one)

    def finish(t, out):
        total[...] = combine(t, z)

        def add(src):
            home_copy(t, src, z).wait_recv()
            total[...] += home[t, src].astype(F32)

        others(side, z, add)
        out[...] = total[...].astype(BF16)

    def token_step(d):
        arrive(0, d)

        @pl.when(d > 0)
        def _():
            @pl.when(d == 1)
            def _():
                for load in loads[2:]:
                    load.wait()
            visit(d - 1, forward)

    def grad_step(d):
        arrive(1, d)

        @pl.when(d == 0)
        def _():
            visit(side - 1, forward)

        @pl.when(d > 0)
        def _():
            visit(d - 1, lambda block: slots_in(1, block))
            visit(d - 1, backward)
            deliver(0, d)

    loop(0, side, token_step)
    loads[1].wait()
    loop(0, side, grad_step)
    visit(side - 1, lambda block: slots_in(1, block))
    share_out(2)
    visit(side - 1, backward)
    share_out(0)
    share_out(1)
    loop(1, side, lambda d: deliver(1, d))
    finish(0, mixed_ref)
    for kind in (2, 0, 1):
        keep_own(kind)
    finish(1, lgrad_ref)

    for kind in range(3):
        others(nd, dp, lambda j: dp_copy(kind, j, dp).wait_recv())
        own_share(kind).wait()
        others(nd, dp, lambda j: dp_copy(kind, dp, j).wait_send())
    others(side, z, lambda k: meta_copy(z, k).wait_send())
    for t in range(2):
        def line_sent(block):
            @pl.when((block <= z) & (z + 1 < side))
            def _():
                line_copy(t, 0, block, z + 1).wait_send()

            @pl.when((block >= z) & (z > 0))
            def _():
                line_copy(t, 1, block, z - 1).wait_send()

            @pl.when(block != z)
            def _():
                home_copy(t, z, block).wait_send()

            def plane_sent(q):
                slot_copy(t, block, p, q).wait_send()
                back_copy(t, block, p, q).wait_send()

            others(side, p, plane_sent)

        loop(0, side, line_sent)


def add_parts(mixed_ref, lgrad_ref, gate_parts, up_parts, down_parts, *outs):
    outs[0][...] = mixed_ref[...]
    outs[1][...] = lgrad_ref[...]
    for parts, out in zip((gate_parts, up_parts, down_parts), outs[2:]):
        out[0] = jnp.sum(parts[...].astype(F32), axis=0)


def shards(tokens, routes, route_weights, gate_weight, up_weight, down_weight, cotangent):
    rows, latent = tokens.shape
    top = routes.shape[1]
    ffn = gate_weight.shape[2]
    experts, nd = lax.axis_size("expert"), lax.axis_size("dp")
    side = math.isqrt(experts)
    assert side * side == experts
    capacity = rows * top // experts
    cap = -(-capacity // 16) * 16
    width, share = side * cap, latent // nd
    vmem = pl.BlockSpec(memory_space=pltpu.VMEM)
    hbm = pl.BlockSpec(memory_space=pl.ANY)
    dma = lambda *shape: pltpu.SemaphoreType.DMA(shape)
    row_out = jax.ShapeDtypeStruct((rows, latent), BF16)
    params = functools.partial(pltpu.CompilerParams, vmem_limit_bytes=60 * 1024 * 1024)
    parts = pl.pallas_call(
        functools.partial(kernel, side, nd, capacity, cap),
        out_shape=(
            row_out,
            row_out,
            jax.ShapeDtypeStruct((nd, share, ffn), BF16),
            jax.ShapeDtypeStruct((nd, share, ffn), BF16),
            jax.ShapeDtypeStruct((nd, ffn, share), BF16),
        ),
        in_specs=[vmem] * 2 + [hbm] * 5,
        out_specs=[vmem] * 2 + [hbm] * 3,
        scratch_shapes=[
            pltpu.VMEM((latent, ffn), BF16),
            pltpu.VMEM((latent, ffn), BF16),
            pltpu.VMEM((ffn, latent), BF16),
            pltpu.VMEM((side, 2 * experts, rows), F32),
            pltpu.VMEM((2, side, rows, latent), BF16),
            pltpu.VMEM((2, side, side, cap, latent), BF16),
            pltpu.VMEM((2, side, side, cap, latent), BF16),
            pltpu.VMEM((2, side, side, cap, latent), BF16),
            pltpu.VMEM((2, side, side, cap, latent), BF16),
            pltpu.VMEM((2, side, rows, latent), BF16),
            pltpu.VMEM((2, side, rows, latent), BF16),
            pltpu.VMEM((rows, latent), F32),
            pltpu.VMEM((side, width, ffn), F32),
            pltpu.VMEM((side, width, ffn), F32),
            pltpu.VMEM((side, width, ffn), BF16),
            pltpu.VMEM((side, width, ffn), BF16),
            pltpu.VMEM((side, width, ffn), BF16),
            pltpu.VMEM((nd, share, ffn), BF16),
            pltpu.VMEM((nd, share, ffn), BF16),
            pltpu.VMEM((nd, ffn, share), BF16),
            dma(5), dma(side), dma(side),
            dma(2, 2, side), dma(2, side),
            dma(2, side, side), dma(2, side, side),
            dma(2, side, side), dma(2, side, side),
            dma(2, side), dma(2, side),
            dma(3, nd), dma(3, nd),
        ],
        compiler_params=params(collective_id=0, has_side_effects=True),
    )(
        routes.T, route_weights.T, tokens, cotangent, gate_weight[0], up_weight[0], down_weight[0]
    )
    steps = 4
    return pl.pallas_call(
        add_parts,
        out_shape=(
            row_out,
            row_out,
            jax.ShapeDtypeStruct((1, share, ffn), F32),
            jax.ShapeDtypeStruct((1, share, ffn), F32),
            jax.ShapeDtypeStruct((1, ffn, share), F32),
        ),
        grid=(steps,),
        in_specs=[
            pl.BlockSpec((rows // steps, latent), lambda i: (i, 0)),
            pl.BlockSpec((rows // steps, latent), lambda i: (i, 0)),
            pl.BlockSpec((nd, share // steps, ffn), lambda i: (0, i, 0)),
            pl.BlockSpec((nd, share // steps, ffn), lambda i: (0, i, 0)),
            pl.BlockSpec((nd, ffn // steps, share), lambda i: (0, i, 0)),
        ],
        out_specs=[
            pl.BlockSpec((rows // steps, latent), lambda i: (i, 0)),
            pl.BlockSpec((rows // steps, latent), lambda i: (i, 0)),
            pl.BlockSpec((1, share // steps, ffn), lambda i: (0, i, 0)),
            pl.BlockSpec((1, share // steps, ffn), lambda i: (0, i, 0)),
            pl.BlockSpec((1, ffn // steps, share), lambda i: (0, i, 0)),
        ],
        compiler_params=params(),
    )(*parts)


def solution(mesh):
    rows = P(("dp", "expert"), None)
    per_expert = P("expert", None, None)
    return jax.shard_map(
        shards,
        mesh=mesh,
        in_specs=(rows, rows, rows, per_expert, per_expert, per_expert, rows),
        out_specs=(
            rows, rows, P("expert", "dp", None), P("expert", "dp", None), P("expert", None, "dp")
        ),
        check_vma=False,
    )
```

```python
import functools
import math

import jax
import jax.numpy as jnp
from jax import lax
from jax.experimental import pallas as pl
from jax.experimental.pallas import tpu as pltpu
from jax.sharding import PartitionSpec as P

F32, BF16 = jnp.float32, jnp.bfloat16


def dot(a, b, contract):
    return lax.dot_general(a, b, (contract, ((), ())), preferred_element_type=F32)


ROWS_COLS = ((1,), (0,))
LAST_LAST = ((1,), (1,))
FIRST_FIRST = ((0,), (0,))


def kernel(
    side, nd, capacity, cap,
    routes_ref, weights_ref, tok_hbm, cot_hbm, gate_hbm, up_hbm, down_hbm,
    mixed_ref, lgrad_ref, gate_parts, up_parts, down_parts,
    gate_ref, up_ref, down_ref,
    meta, line, stage, inbox, back_stage, back, part, home, total, gate_pre, up_pre, hid, gate_gp, up_gp,
    dp_gate, dp_up, dp_down,
    load_sem, meta_send, meta_recv, line_send, line_recv, slot_send, slot_recv, back_send,
    back_recv, home_send, home_recv, dp_send, dp_recv,
):
    experts = side * side
    top, rows = routes_ref.shape
    latent, ffn = gate_ref.shape
    share = latent // nd
    width = side * cap
    me = lax.axis_index("expert")
    dp = lax.axis_index("dp")
    z, p = me // side, me % side

    def at_line(k):
        return {"expert": k * side + p}

    def at_plane(k):
        return {"expert": z * side + k}

    def remote(src, dst, send, recv, device):
        return pltpu.make_async_remote_copy(
            src_ref=src, dst_ref=dst, send_sem=send, recv_sem=recv,
            device_id=device, device_id_type=pl.DeviceIdType.MESH,
        )

    def loop(first, last, body):
        def turn(i, carry):
            body(i)
            return carry
        lax.fori_loop(first, last, turn, 0)

    def others(count, mine, body):
        loop(1, count, lambda r: body((mine + r) % count))

    loads = [
        pltpu.make_async_copy(src, dst, load_sem.at[i])
        for i, (src, dst) in enumerate((
            (tok_hbm, line.at[0, z]), (cot_hbm, line.at[1, z]),
            (gate_hbm, gate_ref), (up_hbm, up_ref), (down_hbm, down_ref),
        ))
    ]
    for load in loads:
        load.start()

    barrier = pltpu.get_barrier_semaphore()

    def greet(device):
        pl.semaphore_signal(barrier, inc=1, device_id=device, device_id_type=pl.DeviceIdType.MESH)

    others(side, z, lambda k: greet(at_line(k)))
    others(side, p, lambda k: greet(at_plane(k)))
    others(nd, dp, lambda k: greet({"dp": k}))

    name = lax.broadcasted_iota(jnp.int32, (experts, rows), 0)
    mask = jnp.zeros((experts, rows), F32)
    weight = jnp.zeros((experts, rows), F32)
    for k in range(top):
        named = routes_ref[k : k + 1, :] == name
        mask = jnp.where(named, 1.0, mask)
        weight = jnp.where(named, weights_ref[k : k + 1, :], weight)
    before = lax.broadcasted_iota(jnp.int32, (rows, rows), 0) < lax.broadcasted_iota(
        jnp.int32, (rows, rows), 1
    )
    rank = dot(mask.astype(BF16), jnp.where(before, 1.0, 0.0).astype(BF16), ROWS_COLS)
    kept = jnp.where(rank < float(capacity), mask, 0.0)
    meta[z, 0:experts, :] = jnp.where(kept > 0.0, rank, -1.0)
    meta[z, experts : 2 * experts, :] = weight
    loads[0].wait()
    loads[1].wait()
    pl.semaphore_wait(barrier, 2 * (side - 1) + nd - 1)

    def meta_copy(src, dst):
        return remote(meta.at[src], meta.at[src], meta_send.at[dst], meta_recv.at[src], at_line(dst))

    def line_copy(t, way, block, dst):
        return remote(
            line.at[t, block], line.at[t, block], line_send.at[t, way, block],
            line_recv.at[t, block], at_line(dst),
        )

    def slot_copy(t, block, src, dst):
        return remote(
            stage.at[t, block, dst], inbox.at[t, block, src],
            slot_send.at[t, block, dst], slot_recv.at[t, block, src], at_plane(dst),
        )

    def back_copy(t, block, src, dst):
        return remote(
            back_stage.at[t, block, dst], back.at[t, block, src],
            back_send.at[t, block, dst], back_recv.at[t, block, src], at_plane(dst),
        )

    def home_copy(t, src, dst):
        return remote(
            part.at[t, dst], home.at[t, src], home_send.at[t, dst], home_recv.at[t, src],
            at_line(dst),
        )

    def dp_copy(kind, src, dst):
        out, come = ((dp_gate, gate_parts), (dp_up, up_parts), (dp_down, down_parts))[kind]
        return remote(
            out.at[dst], come.at[src], dp_send.at[kind, dst], dp_recv.at[kind, src], {"dp": dst}
        )

    def own_share(kind):
        out, come = ((dp_gate, gate_parts), (dp_up, up_parts), (dp_down, down_parts))[kind]
        return pltpu.make_async_copy(out.at[dp], come.at[dp], dp_send.at[kind, dp])

    slot_name = lax.broadcasted_iota(jnp.int32, (cap, rows), 0).astype(F32)

    def selector(block):
        hot, scaled = [], []
        for q in range(side):
            ranks = meta[block, pl.ds(z * side + q, 1), :]
            scale = meta[block, pl.ds(experts + z * side + q, 1), :]
            hit = slot_name == ranks
            hot.append(jnp.where(hit, 1.0, 0.0))
            scaled.append(jnp.where(hit, scale, 0.0))
        return jnp.concatenate(hot, axis=0), jnp.concatenate(scaled, axis=0)

    def visit(d, body):
        def one(s):
            block = z - d + 2 * d * s

            @pl.when((block >= 0) & (block < side) & (d + 1 > s))
            def _():
                body(block)
        loop(0, 2, one)

    def pack(t, block):
        hot, scaled = selector(block)
        picked = dot(hot.astype(BF16), line[t, block], ROWS_COLS)
        if t == 1:
            picked = picked * jnp.sum(scaled, axis=1, keepdims=True)
        stage[t, block] = picked.astype(BF16).reshape(side, cap, latent)
        others(side, p, lambda q: slot_copy(t, block, p, q).start())
        inbox[t, block, p] = stage[t, block, p]

    def relay(t, d, start):
        def come(block):
            @pl.when(d > 0)
            def _():
                if t == 0:
                    meta_copy(block, z).wait_recv()
                line_copy(t, 0, block, z).wait_recv()

        @pl.when(z - d >= 0)
        def _():
            come(z - d)

            @pl.when((z + 1 < side) & start)
            def _():
                line_copy(t, 0, z - d, z + 1).start()

        @pl.when(z + d < side)
        def _():
            come(z + d)

            @pl.when((z > 0) & start)
            def _():
                line_copy(t, 1, z + d, z - 1).start()

    def arrive(t, d):
        relay(t, d, True if t == 0 else d > 0)
        if t == 0:
            @pl.when(d == 0)
            def _():
                others(side, z, lambda k: meta_copy(z, k).start())
        visit(d, lambda block: pack(t, block))

    def hand_back(t, block, value):
        back_stage[t, block] = value.astype(BF16).reshape(side, cap, latent)
        others(side, p, lambda q: back_copy(t, block, p, q).start())
        back[t, block, p] = back_stage[t, block, p]

    def slots_in(t, block):
        others(side, p, lambda q: slot_copy(t, block, q, p).wait_recv())

    def forward(block):
        slots_in(0, block)
        inputs = inbox[0, block].reshape(width, latent)
        pre = dot(inputs, gate_ref[...], ROWS_COLS)
        raised = dot(inputs, up_ref[...], ROWS_COLS)
        gate_pre[block] = pre
        up_pre[block] = raised
        hidden = (pre * jax.nn.sigmoid(pre) * raised).astype(BF16)
        hid[block] = hidden
        hand_back(0, block, dot(hidden, down_ref[...], ROWS_COLS))

    def backward(block):
        pre, raised = gate_pre[block], up_pre[block]
        sig = jax.nn.sigmoid(pre)
        grads = inbox[1, block].reshape(width, latent)
        hidden_grad = dot(grads, down_ref[...], LAST_LAST)
        up_g = (hidden_grad * pre * sig).astype(BF16)
        gate_g = (hidden_grad * raised * sig * (1.0 + pre * (1.0 - sig))).astype(BF16)
        up_gp[block] = up_g
        gate_gp[block] = gate_g
        hand_back(
            1, block, dot(gate_g, gate_ref[...], LAST_LAST) + dot(up_g, up_ref[...], LAST_LAST)
        )

    def columns(j):
        return pl.ds(pl.multiple_of(j * share, share), share)

    def weight_part(kind, j):
        flat = lambda value: value.reshape(side * width, value.shape[-1])
        if kind == 2:
            return dot(flat(hid[...]), flat(inbox[1, :, :, :, columns(j)]), FIRST_FIRST).astype(BF16)
        grads = flat((gate_gp if kind == 0 else up_gp)[...])
        return dot(flat(inbox[0, :, :, :, columns(j)]), grads, FIRST_FIRST).astype(BF16)

    def share_out(kind):
        def one(j):
            (dp_gate, dp_up, dp_down)[kind][j] = weight_part(kind, j)
            dp_copy(kind, dp, j).start()
        others(nd, dp, one)

    def keep_own(kind):
        (dp_gate, dp_up, dp_down)[kind][dp] = weight_part(kind, dp)
        own_share(kind).start()

    def combine(t, block):
        others(side, p, lambda q: back_copy(t, block, q, p).wait_recv())
        hot, scaled = selector(block)
        values = back[t, block].reshape(width, latent)
        if t == 1:
            return dot(hot.astype(BF16), values, FIRST_FIRST)
        high = scaled.astype(BF16)
        low = (scaled - high.astype(F32)).astype(BF16)
        return dot(high, values, FIRST_FIRST) + dot(low, values, FIRST_FIRST)

    def deliver(t, d):
        def one(block):
            part[t, block] = combine(t, block).astype(BF16)
            home_copy(t, z, block).start()
        visit(d, one)

    def finish(t, out):
        total[...] = combine(t, z)

        def add(src):
            home_copy(t, src, z).wait_recv()
            total[...] += home[t, src].astype(F32)

        others(side, z, add)
        out[...] = total[...].astype(BF16)

    def backward_at(d):
        visit(d, lambda block: slots_in(1, block))
        visit(d, backward)

    def token_step(d):
        @pl.when(d == side - 1)
        def _():
            relay(1, 0, True)

        arrive(0, d)

        @pl.when(d == 2)
        def _():
            for load in loads[2:]:
                load.wait()

        @pl.when(d >= 2)
        def _():
            visit(d - 2, forward)

    def grad_step(d):
        arrive(1, d)

        @pl.when(d < 2)
        def _():
            visit(side - 2 + d, forward)

        @pl.when(d >= 2)
        def _():
            backward_at(d - 2)
            deliver(0, d - 1)

    loop(0, side, token_step)
    loop(0, side, grad_step)
    backward_at(side - 2)
    visit(side - 1, lambda block: slots_in(1, block))
    share_out(2)
    visit(side - 1, backward)
    share_out(0)
    share_out(1)
    deliver(0, side - 1)
    loop(1, side, lambda d: deliver(1, d))
    finish(0, mixed_ref)
    for kind in (2, 0, 1):
        keep_own(kind)
    finish(1, lgrad_ref)

    for kind in range(3):
        others(nd, dp, lambda j: dp_copy(kind, j, dp).wait_recv())
        own_share(kind).wait()
        others(nd, dp, lambda j: dp_copy(kind, dp, j).wait_send())
    others(side, z, lambda k: meta_copy(z, k).wait_send())
    for t in range(2):
        def line_sent(block):
            @pl.when((block <= z) & (z + 1 < side))
            def _():
                line_copy(t, 0, block, z + 1).wait_send()

            @pl.when((block >= z) & (z > 0))
            def _():
                line_copy(t, 1, block, z - 1).wait_send()

            @pl.when(block != z)
            def _():
                home_copy(t, z, block).wait_send()

            def plane_sent(q):
                slot_copy(t, block, p, q).wait_send()
                back_copy(t, block, p, q).wait_send()

            others(side, p, plane_sent)

        loop(0, side, line_sent)


def add_parts(mixed_ref, lgrad_ref, gate_parts, up_parts, down_parts, *outs):
    outs[0][...] = mixed_ref[...]
    outs[1][...] = lgrad_ref[...]
    for parts, out in zip((gate_parts, up_parts, down_parts), outs[2:]):
        out[0] = jnp.sum(parts[...].astype(F32), axis=0)


def shards(tokens, routes, route_weights, gate_weight, up_weight, down_weight, cotangent):
    rows, latent = tokens.shape
    top = routes.shape[1]
    ffn = gate_weight.shape[2]
    experts, nd = lax.axis_size("expert"), lax.axis_size("dp")
    side = math.isqrt(experts)
    assert side * side == experts
    capacity = rows * top // experts
    cap = -(-capacity // 16) * 16
    width, share = side * cap, latent // nd
    vmem = pl.BlockSpec(memory_space=pltpu.VMEM)
    hbm = pl.BlockSpec(memory_space=pl.ANY)
    dma = lambda *shape: pltpu.SemaphoreType.DMA(shape)
    row_out = jax.ShapeDtypeStruct((rows, latent), BF16)
    params = functools.partial(pltpu.CompilerParams, vmem_limit_bytes=60 * 1024 * 1024)
    parts = pl.pallas_call(
        functools.partial(kernel, side, nd, capacity, cap),
        out_shape=(
            row_out,
            row_out,
            jax.ShapeDtypeStruct((nd, share, ffn), BF16),
            jax.ShapeDtypeStruct((nd, share, ffn), BF16),
            jax.ShapeDtypeStruct((nd, ffn, share), BF16),
        ),
        in_specs=[vmem] * 2 + [hbm] * 5,
        out_specs=[vmem] * 2 + [hbm] * 3,
        scratch_shapes=[
            pltpu.VMEM((latent, ffn), BF16),
            pltpu.VMEM((latent, ffn), BF16),
            pltpu.VMEM((ffn, latent), BF16),
            pltpu.VMEM((side, 2 * experts, rows), F32),
            pltpu.VMEM((2, side, rows, latent), BF16),
            pltpu.VMEM((2, side, side, cap, latent), BF16),
            pltpu.VMEM((2, side, side, cap, latent), BF16),
            pltpu.VMEM((2, side, side, cap, latent), BF16),
            pltpu.VMEM((2, side, side, cap, latent), BF16),
            pltpu.VMEM((2, side, rows, latent), BF16),
            pltpu.VMEM((2, side, rows, latent), BF16),
            pltpu.VMEM((rows, latent), F32),
            pltpu.VMEM((side, width, ffn), F32),
            pltpu.VMEM((side, width, ffn), F32),
            pltpu.VMEM((side, width, ffn), BF16),
            pltpu.VMEM((side, width, ffn), BF16),
            pltpu.VMEM((side, width, ffn), BF16),
            pltpu.VMEM((nd, share, ffn), BF16),
            pltpu.VMEM((nd, share, ffn), BF16),
            pltpu.VMEM((nd, ffn, share), BF16),
            dma(5), dma(side), dma(side),
            dma(2, 2, side), dma(2, side),
            dma(2, side, side), dma(2, side, side),
            dma(2, side, side), dma(2, side, side),
            dma(2, side), dma(2, side),
            dma(3, nd), dma(3, nd),
        ],
        compiler_params=params(collective_id=0, has_side_effects=True),
    )(
        routes.T, route_weights.T, tokens, cotangent, gate_weight[0], up_weight[0], down_weight[0]
    )
    return pl.pallas_call(
        add_parts,
        out_shape=(
            row_out,
            row_out,
            jax.ShapeDtypeStruct((1, share, ffn), F32),
            jax.ShapeDtypeStruct((1, share, ffn), F32),
            jax.ShapeDtypeStruct((1, ffn, share), F32),
        ),
        in_specs=[vmem] * 5,
        out_specs=[vmem] * 5,
        compiler_params=params(),
    )(*parts)


def solution(mesh):
    rows = P(("dp", "expert"), None)
    per_expert = P("expert", None, None)
    return jax.shard_map(
        shards,
        mesh=mesh,
        in_specs=(rows, rows, rows, per_expert, per_expert, per_expert, rows),
        out_specs=(
            rows, rows, P("expert", "dp", None), P("expert", "dp", None), P("expert", None, "dp")
        ),
        check_vma=False,
    )
```
